32 devices in a mesh: energy: 8 (over z, y), atoms: 4 (over x, core).
Axes of the slice: x: 2, y: 2, z: 4, core: 2. Of those that a mesh axis runs over, the one named last changes fastest.
Arguments:
- green: bfloat16 [1024, 32, 288], P('energy', 'atoms'), may hold values from -6 to 6
- superop: bfloat16 [4, 288, 288], replicated, may hold values from -0.1875 to 0.1875
- phonon: bfloat16 [8, 2048], replicated, may hold values from -0.1875 to 0.1875
- owner: int32 [32, 1], P('atoms'), may hold values from 0 to 7; in each aligned block of 8 rows (0 to 7, 8 to 15, ...) at most 4 rows name the same one
- neighbours: int32 [32, 4], P('atoms'), may hold values from -1 to 31, as said below
Outputs:
- self_energy: bfloat16 [1024, 32, 288], P('energy', 'atoms')
The draws below stay inside these ranges and needn't reach their ends.
Inputs may be any that keep to these rules, and one draw needn't show every extreme that they name: `owner`: within each aligned block of 8 atoms (one atom group) no domain holds more than 4 atoms, and some domain holds exactly 4. `neighbours`: each entry is -1 or the index of an atom at most 8 away from the row's atom; some entry lies exactly 8 above its row's atom, in the next atom group.
All inputs are finite; a program needn't handle non-finite values.
Results may differ from the reference program's by a relative error of at most 0.0049.
Values may be sent and summed in bfloat16 or wider, within the bound.
A program may use at most 64 MiB of HBM per device.

```python
import math
import jax
import jax.numpy as jnp
import numpy as np
from jax import lax

C = 288
NE = 1024
K = 4
HALO = 8
CAP = 4
DOMAINS = 8
GROUP_ATOMS = 8
NA = 32


def draw_neighbours(key, part):
    key_dist, key_side, key_count = jax.random.split(jax.random.fold_in(key, 11), 3)
    atom_ids = jnp.arange(NA, dtype=jnp.int32)[:, None]
    distance = jax.random.randint(key_dist, (NA, K), 1, HALO + 1)
    sides = jax.random.randint(key_side, (NA, K), 0, 2) * 2 - 1
    target = atom_ids + distance * sides
    counts = jax.random.randint(key_count, (NA, 1), 1, K + 1)
    slot_ids = jnp.arange(K, dtype=jnp.int32)[None, :]
    edge = GROUP_ATOMS - 1
    forced = (atom_ids == edge) & (slot_ids == 0)
    target = jnp.where(forced, edge + HALO, target)
    keeping = (slot_ids < counts) & (target >= 0) & (target < NA)
    return jnp.where(keeping, target, -1).astype(jnp.int32)


def shard_levels(own_key, extent, shards, smallest, top_value):
    level, own = 1.0, jax.random.fold_in(own_key, 6)
    for axis_at, parts in shards:
        steps = jnp.exp(jax.random.uniform(jax.random.fold_in(own, axis_at), (parts,), jnp.float32, smallest / len(shards), top_value / len(shards)))
        level = level * jnp.repeat(steps, extent[axis_at] // parts).reshape([-1 if axis == axis_at else 1 for axis in range(len(extent))])
    return level


def assign_block(stream_key, own, number, rows, number_of, top, most, skew):
    order = jax.random.permutation(stream_key, number_of)
    heavy_load, usual = load_shares(number_of, rows * top, most, skew, True), load_shares(number_of, rows * top, most, skew, False)
    places = jnp.arange(number_of)

    def named(tallies, rotation):
        used = int((tallies > 0).sum())
        fixed = max(1, used // 4)
        shifted = fixed + (places - fixed + rotation * (used - fixed)) % max(1, number_of - fixed)
        return jnp.zeros((number_of,), jnp.int32).at[order[jnp.where(places < fixed, places, shifted)]].set(jnp.asarray(tallies, jnp.int32))

    tallies = jnp.where(number % 4 == 0, named(heavy_load, number // 4), named(usual, number - number // 4 - 1))
    mixed = jax.random.permutation(jax.random.fold_in(own, 3), number_of)
    giver, taker = mixed[0:number_of // 2 * 2:2], mixed[1:number_of // 2 * 2:2]
    slack = jnp.minimum(tallies[giver] - 1, most - tallies[taker]) // 2
    slack = jnp.where((giver == order[0]) | (taker == order[0]) | (tallies[taker] == 0), 0, jnp.maximum(slack, 0))
    shifted = jax.random.randint(jax.random.fold_in(own, 4), (number_of // 2,), 0, 1 << 20) % (slack + 1)
    tallies = tallies.at[giver].add(-shifted).at[taker].add(shifted)
    items = jnp.searchsorted(jnp.cumsum(tallies), jnp.arange(rows * top), side="right").astype(jnp.int32)
    table = items.reshape(top, rows).T
    table = table[jax.random.permutation(jax.random.fold_in(own, 1), rows)]
    rotation = jax.random.randint(jax.random.fold_in(own, 2), (rows, 1), 0, top)
    return jnp.take_along_axis(table, (jnp.arange(top)[None, :] + rotation) % top, axis=1)


def load_shares(count, total, reach, lean, full):
    weights = [(1 << 20) // math.isqrt(rank ** lean) + 1 for rank in range(1, count + 1)]
    largest = reach if full else min(reach, max(-(-total // count), total * weights[0] // sum(weights)))
    least = 1 if total - largest >= count - 1 else 0
    holding, rest = [largest] + [least] * (count - 1), total - largest - least * (count - 1)
    while rest > 0:
        free = [i for i in range(1, count) if holding[i] < largest] or [i for i in range(1, count) if holding[i] < reach]
        whole, remaining = sum([weights[i] for i in free]), rest
        for i in free:
            addition = min(reach - holding[i], max(1, remaining * weights[i] // whole), rest)
            holding[i] = holding[i] + addition
            rest = rest - addition
    return np.array(holding)


def bell_draw(key, shape, spread, limit, cuts=(), kind=jnp.bfloat16):
    level = shard_levels(key, shape, cuts, -0.22, 0.18) if cuts else 1.0
    entries = jax.random.normal(key, shape, jnp.float32) * spread * level
    return jnp.minimum(jnp.maximum(entries, -limit), limit).astype(kind)


def setup_inputs(seed: int = 0) -> dict:
    keys = jax.random.split(jax.random.key(seed), 6)
    green = bell_draw(keys[0], (NE, NA, C), 1.0, 6.0, ((0, 8), (1, 4)))
    superop = bell_draw(keys[1], (K, C, C), (K * C) ** -0.5, 0.1875)
    phonon = bell_draw(keys[2], (DOMAINS, 2 * NE), NE ** -0.5, 0.1875)
    owner_keys = jax.random.split(jax.random.fold_in(keys[3], 1), NA // GROUP_ATOMS)
    owner_turns = jax.random.permutation(jax.random.fold_in(keys[3], 3), NA // GROUP_ATOMS)
    owner = jax.vmap(lambda own, number: assign_block(jax.random.fold_in(keys[3], 2), own, number, GROUP_ATOMS, DOMAINS, 1, CAP, 2))(owner_keys, owner_turns).reshape((NA, 1))
    neighbours = draw_neighbours(jax.random.fold_in(keys[5], 71), 0)
    return {"green": green, "superop": superop, "phonon": phonon, "owner": owner, "neighbours": neighbours}


def toeplitz_rows(kernel_row, count):
    length = 2 * count
    flipped = kernel_row[::-1]
    tiled = jnp.tile(flipped, count)[: count * (length - 1)]
    return tiled.reshape(count, length - 1)[:, count - 1: 2 * count - 1]


def reference(green, superop, phonon, owner, neighbours):
    present = neighbours >= 0
    target_rows = jnp.where(present, neighbours, 0).astype(jnp.int32)
    summed = jnp.zeros((NE * NA, C), jnp.float32)
    for neighbour_slot in range(K):
        gathered = jnp.take(green, target_rows[:, neighbour_slot], axis=1)
        gathered = jnp.where(present[:, neighbour_slot][None, :, None], gathered, jnp.zeros_like(gathered))
        summed = summed + jnp.dot(gathered.reshape(NE * NA, C), superop[neighbour_slot], preferred_element_type=jnp.float32)
    coupled = summed.reshape(NE, NA, C).astype(jnp.bfloat16)
    per_atom = jnp.transpose(coupled, (1, 0, 2))

    def one_atom(pair_args):
        domain, columns = pair_args
        kernel = toeplitz_rows(phonon[domain], NE)
        return jnp.dot(kernel, columns, preferred_element_type=jnp.float32).astype(jnp.bfloat16)

    per_result = lax.map(one_atom, (owner[:, 0], per_atom))
    return jnp.transpose(per_result, (1, 0, 2))
```

```python
import functools

import jax
import jax.numpy as jnp
from jax import lax
from jax.experimental import pallas as pl
from jax.experimental.pallas import tpu as pltpu
from jax.sharding import PartitionSpec as P

HALO = 8
MESH = pl.DeviceIdType.MESH
F32 = jnp.float32
BF16 = jnp.bfloat16


def chunks_of(comps, step=128):
    return [(at, min(step, comps - at)) for at in range(0, comps, step)]


def dot(a, b):
    return jnp.dot(a, b, preferred_element_type=F32)


def kernel(
    parts, groups,
    green, superop, phonon, owner, neighbours,
    out,
    wide, turned, table, sent, held, back,
    own_sem, halo_send, halo_recv, go_send, go_recv, ret_send, ret_recv,
):
    me = lax.axis_index("energy")
    group = lax.axis_index("atoms")
    has_left, has_right = group > 0, group < groups - 1
    atoms, comps, local = green.shape
    each = atoms // parts
    slots = neighbours.shape[0]
    span = phonon.shape[1]
    count = span // 2
    deep = table.shape[1]
    per = deep // local
    pieces = chunks_of(comps)

    barrier = pltpu.get_barrier_semaphore()
    for step in range(1, parts):
        peer = lax.rem(me + step, parts)
        pl.semaphore_signal(barrier, inc=1, device_id=(peer, group), device_id_type=MESH)

    @pl.when(has_left)
    def _():
        pl.semaphore_signal(barrier, inc=1, device_id=(me, group - 1), device_id_type=MESH)

    @pl.when(has_right)
    def _():
        pl.semaphore_signal(barrier, inc=1, device_id=(me, group + 1), device_id_type=MESH)

    own = pltpu.make_async_copy(green, wide.at[pl.ds(HALO, atoms)], own_sem)
    own.start()
    pl.semaphore_wait(barrier, parts - 1 + jnp.where(has_left, 1, 0) + jnp.where(has_right, 1, 0))

    to_left = pltpu.make_async_remote_copy(
        src_ref=green.at[pl.ds(0, HALO)], dst_ref=wide.at[pl.ds(HALO + atoms, HALO)],
        send_sem=halo_send.at[0], recv_sem=halo_recv.at[0],
        device_id=(me, group - 1), device_id_type=MESH)
    to_right = pltpu.make_async_remote_copy(
        src_ref=green.at[pl.ds(atoms - HALO, HALO)], dst_ref=wide.at[pl.ds(0, HALO)],
        send_sem=halo_send.at[1], recv_sem=halo_recv.at[1],
        device_id=(me, group + 1), device_id_type=MESH)

    @pl.when(has_left)
    def _():
        to_left.start()

    @pl.when(has_right)
    def _():
        to_right.start()

    empty = 2 * HALO + atoms
    wide[empty] = jnp.zeros((comps, local), BF16)
    turned[...] = superop[...].astype(F32).T.astype(BF16)

    for mine in range(each):
        domain = owner[0, me * each + mine]
        named = lax.broadcasted_iota(jnp.int32, phonon.shape, 0) == domain
        line = jnp.sum(jnp.where(named, phonon[...].astype(F32), 0.0), axis=0, keepdims=True)
        first = pltpu.roll(jnp.broadcast_to(line, (8, span)), 0, 1, stride=1, stride_axis=0)
        for at in range(0, deep, 16):
            pair = [pltpu.roll(first, at, 1) if at else first, pltpu.roll(first, at + 8, 1)]
            table[mine, at:at + 16, :] = jnp.concatenate(pair, axis=0).astype(BF16)

    own.wait()

    @pl.when(has_right)
    def _():
        to_left.wait_recv()

    @pl.when(has_left)
    def _():
        to_right.wait_recv()

    def place(atom, slot):
        target = neighbours[slot, atom]
        near = jnp.clip(target - group * atoms + HALO, 0, empty)
        return jnp.where(target >= 0, near, empty)

    def couple(pair, carry):
        picked = jnp.concatenate([
            jnp.concatenate(
                [wide[place(2 * pair, slot)], wide[place(2 * pair + 1, slot)]], axis=1)
            for slot in range(slots)], axis=0)
        total = dot(turned[...], picked).astype(BF16)
        sent[2 * pair] = total[:, :local]
        sent[2 * pair + 1] = total[:, local:]
        return carry

    lax.fori_loop(0, atoms // 2, couple, 0)

    def go(chunk, step):
        at, size = pieces[chunk]
        peer = lax.rem(me + step, parts)
        return pltpu.make_async_remote_copy(
            src_ref=sent.at[pl.ds(peer * each, each), pl.ds(at, size)],
            dst_ref=held.at[pl.ds(me * each, each), pl.ds(at, size)],
            send_sem=go_send.at[chunk, step], recv_sem=go_recv.at[chunk, step],
            device_id=(peer, group), device_id_type=MESH,
        )

    def ret(chunk, step):
        at, size = pieces[chunk]
        peer = lax.rem(me + step, parts)
        return pltpu.make_async_remote_copy(
            src_ref=back.at[pl.ds(peer * each, each), pl.ds(at, size)],
            dst_ref=out.at[pl.ds(me * each, each), pl.ds(at, size)],
            send_sem=ret_send.at[chunk, step], recv_sem=ret_recv.at[chunk, step],
            device_id=(peer, group), device_id_type=MESH,
        )

    for chunk in range(len(pieces)):
        for step in range(1, parts):
            go(chunk, step).start()
    here = pl.ds(me * each, each)
    held[here] = sent[here]

    for chunk, (at, size) in enumerate(pieces):
        for step in range(1, parts):
            go(chunk, step).wait_recv()
        for mine in range(each):
            total = jnp.zeros((size, count), F32)
            for depth in range(count // deep):
                columns = jnp.concatenate(
                    [held[(depth * per + i) * each + mine, at:at + size, :] for i in range(per)],
                    axis=1)
                first = count - deep * depth
                total = total + dot(columns, table[mine, :, first:first + count])
            total = total.astype(BF16)
            for part in range(parts):
                back[part * each + mine, at:at + size, :] = total[:, part * local:(part + 1) * local]
        for step in range(1, parts):
            ret(chunk, step).start()
        out[here, at:at + size, :] = back[here, at:at + size, :]

    @pl.when(has_left)
    def _():
        to_left.wait_send()

    @pl.when(has_right)
    def _():
        to_right.wait_send()

    for chunk in range(len(pieces)):
        for step in range(1, parts):
            go(chunk, step).wait_send()
    for chunk in range(len(pieces)):
        for step in range(1, parts):
            ret(chunk, step).wait()


def solution(mesh):
    parts, groups = mesh.shape["energy"], mesh.shape["atoms"]

    def per_device(green, superop, phonon, owner, neighbours):
        local, atoms, comps = green.shape
        slots = neighbours.shape[1]
        pieces = len(chunks_of(comps))
        vmem, smem = pl.BlockSpec(memory_space=pltpu.VMEM), pl.BlockSpec(memory_space=pltpu.SMEM)
        result = pl.pallas_call(
            functools.partial(kernel, parts, groups),
            out_shape=jax.ShapeDtypeStruct((atoms, comps, local), BF16),
            in_specs=[pl.BlockSpec(memory_space=pl.ANY), vmem, vmem, smem, smem],
            out_specs=vmem,
            scratch_shapes=[
                pltpu.VMEM((atoms + 2 * HALO + 1, comps, local), BF16),
                pltpu.VMEM((comps, slots * comps), BF16),
                pltpu.VMEM((atoms // parts, 2 * local, phonon.shape[1]), BF16),
                pltpu.VMEM((atoms, comps, local), BF16),
                pltpu.VMEM((atoms, comps, local), BF16),
                pltpu.VMEM((atoms, comps, local), BF16),
                pltpu.SemaphoreType.DMA,
                pltpu.SemaphoreType.DMA((2,)),
                pltpu.SemaphoreType.DMA((2,)),
                pltpu.SemaphoreType.DMA((pieces, parts)),
                pltpu.SemaphoreType.DMA((pieces, parts)),
                pltpu.SemaphoreType.DMA((pieces, parts)),
                pltpu.SemaphoreType.DMA((pieces, parts)),
            ],
            compiler_params=pltpu.CompilerParams(
                collective_id=0, has_side_effects=True, vmem_limit_bytes=48 * 1024 * 1024
            ),
        )(jnp.transpose(green, (1, 2, 0)), superop.reshape(slots * comps, comps), phonon,
          owner.T, neighbours.T)
        return jnp.transpose(result, (2, 0, 1))

    return jax.shard_map(
        per_device,
        mesh=mesh,
        in_specs=(P("energy", "atoms", None), P(), P(), P("atoms", None), P("atoms", None)),
        out_specs=P("energy", "atoms", None),
        check_vma=False,
    )
```

```python
import functools

import jax
import jax.numpy as jnp
from jax import lax
from jax.experimental import pallas as pl
from jax.experimental.pallas import tpu as pltpu
from jax.sharding import PartitionSpec as P

HALO = 8
MESH = pl.DeviceIdType.MESH
F32 = jnp.float32
BF16 = jnp.bfloat16


def chunks_of(comps, step=128):
    return [(at, min(step, comps - at)) for at in range(0, comps, step)]


def dot(a, b):
    return jnp.dot(a, b, preferred_element_type=F32)


def kernel(
    parts, groups,
    green, superop_hbm, phonon_hbm, owner_hbm, neighbours_hbm,
    out,
    superop, phonon, owner, neighbours, wide, turned, table, sent, held, back,
    own_sem, load_sem, halo_send, halo_recv, go_send, go_recv, ret_send, ret_recv,
):
    me = lax.axis_index("energy")
    group = lax.axis_index("atoms")
    has_left, has_right = group > 0, group < groups - 1
    atoms, comps, local = green.shape
    each = atoms // parts
    slots = neighbours.shape[0]
    span = phonon.shape[1]
    count = span // 2
    deep = table.shape[1]
    per = deep // local
    pieces = chunks_of(comps)

    loads = [
        pltpu.make_async_copy(source, target, load_sem.at[i])
        for i, (source, target) in enumerate([
            (superop_hbm, superop), (phonon_hbm, phonon), (owner_hbm, owner),
            (neighbours_hbm, neighbours)])
    ]
    for load in loads:
        load.start()

    barrier = pltpu.get_barrier_semaphore()
    for step in range(1, parts):
        peer = lax.rem(me + step, parts)
        pl.semaphore_signal(barrier, inc=1, device_id=(peer, group), device_id_type=MESH)

    @pl.when(has_left)
    def _():
        pl.semaphore_signal(barrier, inc=1, device_id=(me, group - 1), device_id_type=MESH)

    @pl.when(has_right)
    def _():
        pl.semaphore_signal(barrier, inc=1, device_id=(me, group + 1), device_id_type=MESH)

    own = pltpu.make_async_copy(green, wide.at[pl.ds(HALO, atoms)], own_sem)
    own.start()
    pl.semaphore_wait(barrier, parts - 1 + jnp.where(has_left, 1, 0) + jnp.where(has_right, 1, 0))

    to_left = pltpu.make_async_remote_copy(
        src_ref=green.at[pl.ds(0, HALO)], dst_ref=wide.at[pl.ds(HALO + atoms, HALO)],
        send_sem=halo_send.at[0], recv_sem=halo_recv.at[0],
        device_id=(me, group - 1), device_id_type=MESH)
    to_right = pltpu.make_async_remote_copy(
        src_ref=green.at[pl.ds(atoms - HALO, HALO)], dst_ref=wide.at[pl.ds(0, HALO)],
        send_sem=halo_send.at[1], recv_sem=halo_recv.at[1],
        device_id=(me, group + 1), device_id_type=MESH)

    @pl.when(has_left)
    def _():
        to_left.start()

    @pl.when(has_right)
    def _():
        to_right.start()

    empty = 2 * HALO + atoms
    wide[empty] = jnp.zeros((comps, local), BF16)
    for load in loads:
        load.wait()
    turned[...] = superop[...].astype(F32).T.astype(BF16)

    for mine in range(each):
        domain = owner[0, me * each + mine]
        named = lax.broadcasted_iota(jnp.int32, phonon.shape, 0) == domain
        line = jnp.sum(jnp.where(named, phonon[...].astype(F32), 0.0), axis=0, keepdims=True)
        first = pltpu.roll(jnp.broadcast_to(line, (8, span)), 0, 1, stride=1, stride_axis=0)
        for at in range(0, deep, 16):
            pair = [pltpu.roll(first, at, 1) if at else first, pltpu.roll(first, at + 8, 1)]
            table[mine, at:at + 16, :] = jnp.concatenate(pair, axis=0).astype(BF16)

    own.wait()

    @pl.when(has_right)
    def _():
        to_left.wait_recv()

    @pl.when(has_left)
    def _():
        to_right.wait_recv()

    def place(atom, slot):
        target = neighbours[slot, atom]
        near = jnp.clip(target - group * atoms + HALO, 0, empty)
        return jnp.where(target >= 0, near, empty)

    def go(chunk, step):
        at, size = pieces[chunk]
        peer = lax.rem(me + step, parts)
        return pltpu.make_async_remote_copy(
            src_ref=sent.at[pl.ds(peer * each, each), pl.ds(at, size)],
            dst_ref=held.at[pl.ds(me * each, each), pl.ds(at, size)],
            send_sem=go_send.at[chunk, step], recv_sem=go_recv.at[chunk, step],
            device_id=(peer, group), device_id_type=MESH,
        )

    def ret(chunk, step):
        at, size = pieces[chunk]
        peer = lax.rem(me + step, parts)
        return pltpu.make_async_remote_copy(
            src_ref=back.at[pl.ds(peer * each, each), pl.ds(at, size)],
            dst_ref=out.at[pl.ds(me * each, each), pl.ds(at, size)],
            send_sem=ret_send.at[chunk, step], recv_sem=ret_recv.at[chunk, step],
            device_id=(peer, group), device_id_type=MESH,
        )

    unit = max(each, 2)
    units = atoms // unit

    def couple(turn, carry):
        at_unit = lax.rem(me * each // unit + units // 2 + turn, units)
        base = at_unit * unit
        for first in range(0, unit, 2):
            picked = jnp.concatenate([
                jnp.concatenate(
                    [wide[place(base + first, slot)], wide[place(base + first + 1, slot)]], axis=1)
                for slot in range(slots)], axis=0)
            total = dot(turned[...], picked).astype(BF16)
            sent[base + first] = total[:, :local]
            sent[base + first + 1] = total[:, local:]
        for which in range(unit // each):
            peer = at_unit * (unit // each) + which

            @pl.when(peer != me)
            def _(peer=peer):
                go(0, lax.rem(peer - me + parts, parts)).start()
        return carry

    lax.fori_loop(0, units, couple, 0)

    far_first = sorted(range(1, parts), key=lambda step: abs(step - parts // 2))
    for chunk in range(1, len(pieces)):
        for step in far_first:
            go(chunk, step).start()
    here = pl.ds(me * each, each)
    held[here] = sent[here]

    for chunk, (at, size) in enumerate(pieces):
        for step in range(1, parts):
            go(chunk, step).wait_recv()
        for mine in range(each):
            total = jnp.zeros((size, count), F32)
            for depth in range(count // deep):
                columns = jnp.concatenate(
                    [held[(depth * per + i) * each + mine, at:at + size, :] for i in range(per)],
                    axis=1)
                first = count - deep * depth
                total = total + dot(columns, table[mine, :, first:first + count])
            total = total.astype(BF16)
            for part in range(parts):
                back[part * each + mine, at:at + size, :] = total[:, part * local:(part + 1) * local]
        for step in far_first:
            ret(chunk, step).start()
        out[here, at:at + size, :] = back[here, at:at + size, :]

    @pl.when(has_left)
    def _():
        to_left.wait_send()

    @pl.when(has_right)
    def _():
        to_right.wait_send()

    for chunk in range(len(pieces)):
        for step in range(1, parts):
            go(chunk, step).wait_send()
    for chunk in range(len(pieces)):
        for step in range(1, parts):
            ret(chunk, step).wait()


def solution(mesh):
    parts, groups = mesh.shape["energy"], mesh.shape["atoms"]

    def per_device(green, superop, phonon, owner, neighbours):
        local, atoms, comps = green.shape
        slots = neighbours.shape[1]
        pieces = len(chunks_of(comps))
        hbm = pl.BlockSpec(memory_space=pltpu.HBM)
        result = pl.pallas_call(
            functools.partial(kernel, parts, groups),
            out_shape=jax.ShapeDtypeStruct((atoms, comps, local), BF16),
            in_specs=[hbm] * 5,
            out_specs=pl.BlockSpec(memory_space=pltpu.VMEM),
            scratch_shapes=[
                pltpu.VMEM((slots * comps, comps), BF16),
                pltpu.VMEM(phonon.shape, BF16),
                pltpu.SMEM((1, atoms), jnp.int32),
                pltpu.SMEM((slots, atoms), jnp.int32),
                pltpu.VMEM((atoms + 2 * HALO + 1, comps, local), BF16),
                pltpu.VMEM((comps, slots * comps), BF16),
                pltpu.VMEM((atoms // parts, 2 * local, phonon.shape[1]), BF16),
                pltpu.VMEM((atoms, comps, local), BF16),
                pltpu.VMEM((atoms, comps, local), BF16),
                pltpu.VMEM((atoms, comps, local), BF16),
                pltpu.SemaphoreType.DMA,
                pltpu.SemaphoreType.DMA((4,)),
                pltpu.SemaphoreType.DMA((2,)),
                pltpu.SemaphoreType.DMA((2,)),
                pltpu.SemaphoreType.DMA((pieces, parts)),
                pltpu.SemaphoreType.DMA((pieces, parts)),
                pltpu.SemaphoreType.DMA((pieces, parts)),
                pltpu.SemaphoreType.DMA((pieces, parts)),
            ],
            compiler_params=pltpu.CompilerParams(
                collective_id=0, has_side_effects=True, vmem_limit_bytes=60 * 1024 * 1024
            ),
        )(jnp.transpose(green, (1, 2, 0)), superop.reshape(slots * comps, comps), phonon,
          owner.T, neighbours.T)
        return jnp.transpose(result, (2, 0, 1))

    return jax.shard_map(
        per_device,
        mesh=mesh,
        in_specs=(P("energy", "atoms", None), P(), P(), P("atoms", None), P("atoms", None)),
        out_specs=P("energy", "atoms", None),
        check_vma=False,
    )
```

```python
import functools

import jax
import jax.numpy as jnp
from jax import lax
from jax.experimental import pallas as pl
from jax.experimental.pallas import tpu as pltpu
from jax.sharding import PartitionSpec as P

HALO = 8
MESH = pl.DeviceIdType.MESH
F32 = jnp.float32
BF16 = jnp.bfloat16


def chunks_of(comps, step=96):
    return [(at, min(step, comps - at)) for at in range(0, comps, step)]


def dot(a, b):
    return jnp.dot(a, b, preferred_element_type=F32)


def kernel(
    parts, groups,
    green, superop_hbm, phonon_hbm, owner_hbm, neighbours_hbm,
    out,
    superop, phonon, owner, neighbours, wide, turned, table, sent, held, back,
    own_sem, load_sem, halo_send, halo_recv, go_send, go_recv, ret_send, ret_recv,
):
    me = lax.axis_index("energy")
    group = lax.axis_index("atoms")
    has_left, has_right = group > 0, group < groups - 1
    atoms, comps, local = green.shape
    each = atoms // parts
    slots = neighbours.shape[0]
    span = phonon.shape[1]
    count = span // 2
    deep = table.shape[1]
    per = deep // local
    pieces = chunks_of(comps)

    loads = [
        pltpu.make_async_copy(source, target, load_sem.at[i])
        for i, (source, target) in enumerate([
            (superop_hbm, superop), (phonon_hbm, phonon), (owner_hbm, owner),
            (neighbours_hbm, neighbours)])
    ]
    for load in loads:
        load.start()

    barrier = pltpu.get_barrier_semaphore()
    for step in range(1, parts):
        peer = lax.rem(me + step, parts)
        pl.semaphore_signal(barrier, inc=1, device_id=(peer, group), device_id_type=MESH)

    @pl.when(has_left)
    def _():
        pl.semaphore_signal(barrier, inc=1, device_id=(me, group - 1), device_id_type=MESH)

    @pl.when(has_right)
    def _():
        pl.semaphore_signal(barrier, inc=1, device_id=(me, group + 1), device_id_type=MESH)

    own = pltpu.make_async_copy(green, wide.at[pl.ds(HALO, atoms)], own_sem)
    own.start()
    pl.semaphore_wait(barrier, parts - 1 + jnp.where(has_left, 1, 0) + jnp.where(has_right, 1, 0))

    to_left = pltpu.make_async_remote_copy(
        src_ref=green.at[pl.ds(0, HALO)], dst_ref=wide.at[pl.ds(HALO + atoms, HALO)],
        send_sem=halo_send.at[0], recv_sem=halo_recv.at[0],
        device_id=(me, group - 1), device_id_type=MESH)
    to_right = pltpu.make_async_remote_copy(
        src_ref=green.at[pl.ds(atoms - HALO, HALO)], dst_ref=wide.at[pl.ds(0, HALO)],
        send_sem=halo_send.at[1], recv_sem=halo_recv.at[1],
        device_id=(me, group + 1), device_id_type=MESH)

    @pl.when(has_left)
    def _():
        to_left.start()

    @pl.when(has_right)
    def _():
        to_right.start()

    empty = 2 * HALO + atoms
    wide[empty] = jnp.zeros((comps, local), BF16)
    for load in loads:
        load.wait()
    turned[...] = superop[...].astype(F32).T.astype(BF16)

    own.wait()

    @pl.when(has_right)
    def _():
        to_left.wait_recv()

    @pl.when(has_left)
    def _():
        to_right.wait_recv()

    def place(atom, slot):
        target = neighbours[slot, atom]
        near = jnp.clip(target - group * atoms + HALO, 0, empty)
        return jnp.where(target >= 0, near, empty)

    def go(chunk, step):
        at, size = pieces[chunk]
        peer = lax.rem(me + step, parts)
        return pltpu.make_async_remote_copy(
            src_ref=sent.at[pl.ds(peer * each, each), pl.ds(at, size)],
            dst_ref=held.at[pl.ds(me * each, each), pl.ds(at, size)],
            send_sem=go_send.at[chunk, step], recv_sem=go_recv.at[chunk, step],
            device_id=(peer, group), device_id_type=MESH,
        )

    def ret(chunk, step):
        at, size = pieces[chunk]
        peer = lax.rem(me + step, parts)
        return pltpu.make_async_remote_copy(
            src_ref=back.at[pl.ds(peer * each, each), pl.ds(at, size)],
            dst_ref=out.at[pl.ds(me * each, each), pl.ds(at, size)],
            send_sem=ret_send.at[chunk, step], recv_sem=ret_recv.at[chunk, step],
            device_id=(peer, group), device_id_type=MESH,
        )

    unit = max(each, 2)
    units = atoms // unit

    def couple(turn, carry):
        at_unit = lax.rem(me * each // unit + units // 2 + turn, units)
        base = at_unit * unit
        for first in range(0, unit, 2):
            picked = jnp.concatenate([
                jnp.concatenate(
                    [wide[place(base + first, slot)], wide[place(base + first + 1, slot)]], axis=1)
                for slot in range(slots)], axis=0)
            total = dot(turned[...], picked).astype(BF16)
            sent[base + first] = total[:, :local]
            sent[base + first + 1] = total[:, local:]
        for which in range(unit // each):
            peer = at_unit * (unit // each) + which

            @pl.when(peer != me)
            def _(peer=peer):
                go(0, lax.rem(peer - me + parts, parts)).start()
        return carry

    lax.fori_loop(0, units, couple, 0)

    far_first = sorted(range(1, parts), key=lambda step: abs(step - parts // 2))
    def kept(chunk):
        at, size = pieces[chunk]
        here = pl.ds(me * each, each), pl.ds(at, size)
        return pltpu.make_async_copy(back.at[here], out.at[here], ret_send.at[chunk, 0])

    for chunk in range(1, len(pieces)):
        for step in far_first:
            go(chunk, step).start()
    here = pl.ds(me * each, each)
    held[here] = sent[here]

    for mine in range(each):
        domain = owner[0, me * each + mine]
        named = lax.broadcasted_iota(jnp.int32, phonon.shape, 0) == domain
        line = jnp.sum(jnp.where(named, phonon[...].astype(F32), 0.0), axis=0, keepdims=True)
        first = pltpu.roll(jnp.broadcast_to(line, (8, span)), 0, 1, stride=1, stride_axis=0)
        for at in range(0, deep, 16):
            pair = [pltpu.roll(first, at, 1) if at else first, pltpu.roll(first, at + 8, 1)]
            table[mine, at:at + 16, :] = jnp.concatenate(pair, axis=0).astype(BF16)

    for chunk, (at, size) in enumerate(pieces):
        for step in range(1, parts):
            go(chunk, step).wait_recv()
        for mine in range(each):
            total = jnp.zeros((size, count), F32)
            for depth in range(count // deep):
                columns = jnp.concatenate(
                    [held[(depth * per + i) * each + mine, at:at + size, :] for i in range(per)],
                    axis=1)
                first = count - deep * depth
                total = total + dot(columns, table[mine, :, first:first + count])
            total = total.astype(BF16)
            for part in range(parts):
                back[part * each + mine, at:at + size, :] = total[:, part * local:(part + 1) * local]
        for step in far_first:
            ret(chunk, step).start()
        kept(chunk).start()

    @pl.when(has_left)
    def _():
        to_left.wait_send()

    @pl.when(has_right)
    def _():
        to_right.wait_send()

    for chunk in range(len(pieces)):
        for step in range(1, parts):
            go(chunk, step).wait_send()
    for chunk in range(len(pieces)):
        kept(chunk).wait()
        for step in range(1, parts):
            ret(chunk, step).wait()


def solution(mesh):
    parts, groups = mesh.shape["energy"], mesh.shape["atoms"]

    def per_device(green, superop, phonon, owner, neighbours):
        local, atoms, comps = green.shape
        slots = neighbours.shape[1]
        pieces = len(chunks_of(comps))
        hbm = pl.BlockSpec(memory_space=pltpu.HBM)
        result = pl.pallas_call(
            functools.partial(kernel, parts, groups),
            out_shape=jax.ShapeDtypeStruct((atoms, comps, local), BF16),
            in_specs=[hbm] * 5,
            out_specs=hbm,
            scratch_shapes=[
                pltpu.VMEM((slots * comps, comps), BF16),
                pltpu.VMEM(phonon.shape, BF16),
                pltpu.SMEM((1, atoms), jnp.int32),
                pltpu.SMEM((slots, atoms), jnp.int32),
                pltpu.VMEM((atoms + 2 * HALO + 1, comps, local), BF16),
                pltpu.VMEM((comps, slots * comps), BF16),
                pltpu.VMEM((atoms // parts, 2 * local, phonon.shape[1]), BF16),
                pltpu.VMEM((atoms, comps, local), BF16),
                pltpu.VMEM((atoms, comps, local), BF16),
                pltpu.VMEM((atoms, comps, local), BF16),
                pltpu.SemaphoreType.DMA,
                pltpu.SemaphoreType.DMA((4,)),
                pltpu.SemaphoreType.DMA((2,)),
                pltpu.SemaphoreType.DMA((2,)),
                pltpu.SemaphoreType.DMA((pieces, parts)),
                pltpu.SemaphoreType.DMA((pieces, parts)),
                pltpu.SemaphoreType.DMA((pieces, parts)),
                pltpu.SemaphoreType.DMA((pieces, parts)),
            ],
            compiler_params=pltpu.CompilerParams(
                collective_id=0, has_side_effects=True, vmem_limit_bytes=60 * 1024 * 1024
            ),
        )(jnp.transpose(green, (1, 2, 0)), superop.reshape(slots * comps, comps), phonon,
          owner.T, neighbours.T)
        return jnp.transpose(result, (2, 0, 1))

    return jax.shard_map(
        per_device,
        mesh=mesh,
        in_specs=(P("energy", "atoms", None), P(), P(), P("atoms", None), P("atoms", None)),
        out_specs=P("energy", "atoms", None),
        check_vma=False,
    )
```

```python
import functools

import jax
import jax.numpy as jnp
from jax import lax
from jax.experimental import pallas as pl
from jax.experimental.pallas import tpu as pltpu
from jax.sharding import PartitionSpec as P

HALO = 8
MESH = pl.DeviceIdType.MESH
F32 = jnp.float32
BF16 = jnp.bfloat16


def chunks_of(comps, step=112):
    return [(at, min(step, comps - at)) for at in range(0, comps, step)]


def dot(a, b):
    return jnp.dot(a, b, preferred_element_type=F32)


def kernel(
    parts, groups,
    green, superop_hbm, phonon_hbm, owner_hbm, neighbours_hbm,
    out,
    superop, phonon, owner, neighbours, wide, turned, table, sent, held, back,
    own_sem, load_sem, halo_send, halo_recv, go_send, go_recv, ret_send, ret_recv,
):
    me = lax.axis_index("energy")
    group = lax.axis_index("atoms")
    has_left, has_right = group > 0, group < groups - 1
    atoms, comps, local = green.shape
    each = atoms // parts
    slots = neighbours.shape[0]
    span = phonon.shape[1]
    count = span // 2
    deep = table.shape[1]
    per = deep // local
    pieces = chunks_of(comps)

    loads = [
        pltpu.make_async_copy(source, target, load_sem.at[i])
        for i, (source, target) in enumerate([
            (superop_hbm, superop), (phonon_hbm, phonon), (owner_hbm, owner),
            (neighbours_hbm, neighbours)])
    ]
    for load in loads:
        load.start()

    barrier = pltpu.get_barrier_semaphore()
    for step in range(1, parts):
        peer = lax.rem(me + step, parts)
        pl.semaphore_signal(barrier, inc=1, device_id=(peer, group), device_id_type=MESH)

    @pl.when(has_left)
    def _():
        pl.semaphore_signal(barrier, inc=1, device_id=(me, group - 1), device_id_type=MESH)

    @pl.when(has_right)
    def _():
        pl.semaphore_signal(barrier, inc=1, device_id=(me, group + 1), device_id_type=MESH)

    own = pltpu.make_async_copy(green, wide.at[pl.ds(HALO, atoms)], own_sem)
    own.start()
    pl.semaphore_wait(barrier, parts - 1 + jnp.where(has_left, 1, 0) + jnp.where(has_right, 1, 0))

    to_left = pltpu.make_async_remote_copy(
        src_ref=green.at[pl.ds(0, HALO)], dst_ref=wide.at[pl.ds(HALO + atoms, HALO)],
        send_sem=halo_send.at[0], recv_sem=halo_recv.at[0],
        device_id=(me, group - 1), device_id_type=MESH)
    to_right = pltpu.make_async_remote_copy(
        src_ref=green.at[pl.ds(atoms - HALO, HALO)], dst_ref=wide.at[pl.ds(0, HALO)],
        send_sem=halo_send.at[1], recv_sem=halo_recv.at[1],
        device_id=(me, group + 1), device_id_type=MESH)

    @pl.when(has_left)
    def _():
        to_left.start()

    @pl.when(has_right)
    def _():
        to_right.start()

    empty = 2 * HALO + atoms
    wide[empty] = jnp.zeros((comps, local), BF16)
    for load in loads:
        load.wait()
    turned[...] = superop[...].astype(F32).T.astype(BF16)

    own.wait()

    @pl.when(has_right)
    def _():
        to_left.wait_recv()

    @pl.when(has_left)
    def _():
        to_right.wait_recv()

    def place(atom, slot):
        target = neighbours[slot, atom]
        near = jnp.clip(target - group * atoms + HALO, 0, empty)
        return jnp.where(target >= 0, near, empty)

    def go(chunk, step):
        at, size = pieces[chunk]
        peer = lax.rem(me + step, parts)
        return pltpu.make_async_remote_copy(
            src_ref=sent.at[pl.ds(peer * each, each), pl.ds(at, size)],
            dst_ref=held.at[pl.ds(me * each, each), pl.ds(at, size)],
            send_sem=go_send.at[chunk, step], recv_sem=go_recv.at[chunk, step],
            device_id=(peer, group), device_id_type=MESH,
        )

    def ret(chunk, step):
        at, size = pieces[chunk]
        peer = lax.rem(me + step, parts)
        return pltpu.make_async_remote_copy(
            src_ref=back.at[pl.ds(peer * each, each), pl.ds(at, size)],
            dst_ref=out.at[pl.ds(me * each, each), pl.ds(at, size)],
            send_sem=ret_send.at[chunk, step], recv_sem=ret_recv.at[chunk, step],
            device_id=(peer, group), device_id_type=MESH,
        )

    unit = max(each, 2)
    units = atoms // unit

    def couple(turn, carry):
        at_unit = lax.rem(me * each // unit + units // 2 + turn, units)
        base = at_unit * unit
        for first in range(0, unit, 2):
            picked = jnp.concatenate([
                jnp.concatenate(
                    [wide[place(base + first, slot)], wide[place(base + first + 1, slot)]], axis=1)
                for slot in range(slots)], axis=0)
            total = dot(turned[...], picked).astype(BF16)
            sent[base + first] = total[:, :local]
            sent[base + first + 1] = total[:, local:]
        for which in range(unit // each):
            peer = at_unit * (unit // each) + which

            @pl.when(peer != me)
            def _(peer=peer):
                go(0, lax.rem(peer - me + parts, parts)).start()
        return carry

    lax.fori_loop(0, units, couple, 0)

    far_first = sorted(range(1, parts), key=lambda step: abs(step - parts // 2))
    def kept(chunk):
        at, size = pieces[chunk]
        here = pl.ds(me * each, each), pl.ds(at, size)
        return pltpu.make_async_copy(back.at[here], out.at[here], ret_send.at[chunk, 0])

    for chunk in range(1, len(pieces)):
        for step in far_first:
            go(chunk, step).start()
    here = pl.ds(me * each, each)
    held[here] = sent[here]

    for mine in range(each):
        domain = owner[0, me * each + mine]
        named = lax.broadcasted_iota(jnp.int32, phonon.shape, 0) == domain
        line = jnp.sum(jnp.where(named, phonon[...].astype(F32), 0.0), axis=0, keepdims=True)
        first = pltpu.roll(jnp.broadcast_to(line, (8, span)), 0, 1, stride=1, stride_axis=0)
        for at in range(0, deep, 16):
            pair = [pltpu.roll(first, at, 1) if at else first, pltpu.roll(first, at + 8, 1)]
            table[mine, at:at + 16, :] = jnp.concatenate(pair, axis=0).astype(BF16)

    for chunk, (at, size) in enumerate(pieces):
        for step in range(1, parts):
            go(chunk, step).wait_recv()
        for mine in range(each):
            total = jnp.zeros((size, count), F32)
            for depth in range(count // deep):
                columns = jnp.concatenate(
                    [held[(depth * per + i) * each + mine, at:at + size, :] for i in range(per)],
                    axis=1)
                first = count - deep * depth
                total = total + dot(columns, table[mine, :, first:first + count])
            total = total.astype(BF16)
            for part in range(parts):
                back[part * each + mine, at:at + size, :] = total[:, part * local:(part + 1) * local]
        for step in far_first:
            ret(chunk, step).start()
        kept(chunk).start()

    @pl.when(has_left)
    def _():
        to_left.wait_send()

    @pl.when(has_right)
    def _():
        to_right.wait_send()

    for chunk in range(len(pieces)):
        for step in range(1, parts):
            go(chunk, step).wait_send()
    for chunk in range(len(pieces)):
        kept(chunk).wait()
        for step in range(1, parts):
            ret(chunk, step).wait()


def solution(mesh):
    parts, groups = mesh.shape["energy"], mesh.shape["atoms"]

    def per_device(green, superop, phonon, owner, neighbours):
        local, atoms, comps = green.shape
        slots = neighbours.shape[1]
        pieces = len(chunks_of(comps))
        hbm = pl.BlockSpec(memory_space=pltpu.HBM)
        result = pl.pallas_call(
            functools.partial(kernel, parts, groups),
            out_shape=jax.ShapeDtypeStruct((atoms, comps, local), BF16),
            in_specs=[hbm] * 5,
            out_specs=hbm,
            scratch_shapes=[
                pltpu.VMEM((slots * comps, comps), BF16),
                pltpu.VMEM(phonon.shape, BF16),
                pltpu.SMEM((1, atoms), jnp.int32),
                pltpu.SMEM((slots, atoms), jnp.int32),
                pltpu.VMEM((atoms + 2 * HALO + 1, comps, local), BF16),
                pltpu.VMEM((comps, slots * comps), BF16),
                pltpu.VMEM((atoms // parts, 2 * local, phonon.shape[1]), BF16),
                pltpu.VMEM((atoms, comps, local), BF16),
                pltpu.VMEM((atoms, comps, local), BF16),
                pltpu.VMEM((atoms, comps, local), BF16),
                pltpu.SemaphoreType.DMA,
                pltpu.SemaphoreType.DMA((4,)),
                pltpu.SemaphoreType.DMA((2,)),
                pltpu.SemaphoreType.DMA((2,)),
                pltpu.SemaphoreType.DMA((pieces, parts)),
                pltpu.SemaphoreType.DMA((pieces, parts)),
                pltpu.SemaphoreType.DMA((pieces, parts)),
                pltpu.SemaphoreType.DMA((pieces, parts)),
            ],
            compiler_params=pltpu.CompilerParams(
                collective_id=0, has_side_effects=True, vmem_limit_bytes=60 * 1024 * 1024
            ),
        )(jnp.transpose(green, (1, 2, 0)), superop.reshape(slots * comps, comps), phonon,
          owner.T, neighbours.T)
        return jnp.transpose(result, (2, 0, 1))

    return jax.shard_map(
        per_device,
        mesh=mesh,
        in_specs=(P("energy", "atoms", None), P(), P(), P("atoms", None), P("atoms", None)),
        out_specs=P("energy", "atoms", None),
        check_vma=False,
    )
```
